32 devices in a mesh: grp: 4 (over y, x), dev: 8 (over z, core).
Axes of the slice: x: 2, y: 2, z: 4, core: 2. Of those that a mesh axis runs over, the one named last changes fastest.
Arguments:
- blocks: bfloat16 [256, 64, 4096], P(('grp', 'dev')), may hold values from -6 to 6
- coords: int32 [3, 256], P(None, ('grp', 'dev')), may hold values from 0 to 15, as said below
- counts: int32 [32], P(('grp', 'dev')), may hold values from 1 to 8, as said below
- row_place: int32 [16], replicated, may hold values from 0 to 15, as said below
- factor_one: bfloat16 [16, 4096], P('dev'), may hold values from -0.75 to 0.75
- factor_two: bfloat16 [16, 4096], P('dev'), may hold values from -0.75 to 0.75
- factor_three: bfloat16 [16, 4096], P('dev'), may hold values from -0.75 to 0.75
Outputs:
- new_rows: float32 [16, 4096], P('dev')
- gram: float32 [64, 64], replicated
The draws below stay inside these ranges and needn't reach their ends.
Inputs may be any that keep to these rules, and one draw needn't show every extreme that they name: `coords`: every mode-1 id of a slot on the device with dev index d has its row-block position in [d * 2, (d + 1) * 2); on one device, the row-block positions of the mode-2 ids of its 8 slots lie in pairwise different ranges [e * 2, (e + 1) * 2), and so do those of the mode-3 ids. `counts`: some device has all 8 slots live. `row_place`: A permutation of 0 to 15.
All inputs are finite; a program needn't handle non-finite values.
Results may differ from the reference program's by a relative error of at most 0.0056.
Values may be sent and summed in bfloat16 or wider, within the bound.
No kernel may reach another device: no remote copies, remote signals or barrier semaphores. Data moves between devices by JAX's collectives and lax.ppermute only.
A program may use at most 128 MiB of HBM per device.

```python
import jax
import jax.numpy as jnp
from jax import lax

BLOCK_EDGE = 64
R = 64
DEVICE_BLOCKS = 8
DEVICE_ROW_BLOCKS = 2
NRB = 16
TOTAL_SLOTS = 256
N_GRP = 4
N_DEV = 8


def shared_place(key):
    return jax.random.permutation(jax.random.fold_in(key, 7), NRB).astype(jnp.int32)


def draw_row_place(key, part):
    return shared_place(key)


def distinct_owners(key):
    total = N_GRP * N_DEV
    scores = jax.random.randint(key, (total, N_DEV), 0, 4096).astype(jnp.int32)
    scores = scores * N_DEV + jnp.arange(N_DEV).astype(jnp.int32)[None, :]
    sort_order = jnp.argsort(scores, axis=1, stable=True).astype(jnp.int32)
    return sort_order[:, :DEVICE_BLOCKS].reshape(TOTAL_SLOTS)


def draw_coords(key, part):
    place = shared_place(key)
    id_at = jnp.argsort(place).astype(jnp.int32)
    block_index = jnp.arange(TOTAL_SLOTS).astype(jnp.int32)
    dev_index = block_index // DEVICE_BLOCKS % N_DEV
    local_part = jax.random.randint(jax.random.fold_in(key, 11), (TOTAL_SLOTS,), 0, DEVICE_ROW_BLOCKS).astype(jnp.int32)
    ids_one = id_at[dev_index * DEVICE_ROW_BLOCKS + local_part]
    owner_two = distinct_owners(jax.random.fold_in(key, 13))
    owner_three = distinct_owners(jax.random.fold_in(key, 17))
    local_part_two = jax.random.randint(jax.random.fold_in(key, 29), (TOTAL_SLOTS,), 0, DEVICE_ROW_BLOCKS).astype(jnp.int32)
    local_part_three = jax.random.randint(jax.random.fold_in(key, 31), (TOTAL_SLOTS,), 0, DEVICE_ROW_BLOCKS).astype(jnp.int32)
    ids_two = id_at[owner_two * DEVICE_ROW_BLOCKS + local_part_two]
    ids_three = id_at[owner_three * DEVICE_ROW_BLOCKS + local_part_three]
    return jnp.stack([ids_one, ids_two, ids_three], axis=0).astype(jnp.int32)


def draw_counts(key, part):
    total = N_GRP * N_DEV
    values = jax.random.randint(jax.random.fold_in(key, 19), (total,), 1, DEVICE_BLOCKS + 1).astype(jnp.int32)
    fullest = jax.random.randint(jax.random.fold_in(key, 23), (), 0, total)
    return values.at[fullest].set(DEVICE_BLOCKS).astype(jnp.int32)


def level_of(rng, extent, pieces, low, high):
    level, own = 1.0, jax.random.fold_in(rng, 6)
    for axis_at, shards_of in pieces:
        steps = jnp.exp(jax.random.uniform(jax.random.fold_in(own, axis_at), (shards_of,), jnp.float32, low / len(pieces), high / len(pieces)))
        level = level * jnp.repeat(steps, extent[axis_at] // shards_of).reshape([-1 if axis == axis_at else 1 for axis in range(len(extent))])
    return level


def gaussian(rng, dims, spread, limit, split=(), kind=jnp.bfloat16):
    result = spread * jax.random.normal(rng, dims, jnp.float32)
    if split:
        result = result * level_of(rng, dims, split, -0.22, 0.18)
    return jnp.clip(result, -limit, limit).astype(kind)


def setup_inputs(seed: int = 0) -> dict:
    seeds = jax.random.split(jax.random.key(seed), 8)
    return {
        "blocks": gaussian(seeds[0], (TOTAL_SLOTS, BLOCK_EDGE, BLOCK_EDGE * BLOCK_EDGE), 1.0, 6.0, ((0, 32),)),
        "coords": draw_coords(jax.random.fold_in(seeds[7], 71), 0),
        "counts": draw_counts(jax.random.fold_in(seeds[7], 71), 0),
        "row_place": draw_row_place(jax.random.fold_in(seeds[7], 71), 0),
        "factor_one": gaussian(seeds[4], (NRB, BLOCK_EDGE * R), BLOCK_EDGE ** -0.5, 0.75, ((0, 8),)),
        "factor_two": gaussian(seeds[5], (NRB, BLOCK_EDGE * R), BLOCK_EDGE ** -0.5, 0.75, ((0, 8),)),
        "factor_three": gaussian(seeds[6], (NRB, BLOCK_EDGE * R), BLOCK_EDGE ** -0.5, 0.75, ((0, 8),)),
    }


def reference(blocks, coords, counts, row_place, factor_one, factor_two, factor_three):
    slots = blocks.shape[0]
    block_index = jnp.arange(slots).astype(jnp.int32)
    owner = (block_index // DEVICE_BLOCKS).astype(jnp.int32)
    alive = (block_index % DEVICE_BLOCKS < counts[owner]).astype(jnp.float32)
    places = row_place[coords].astype(jnp.int32)

    def advance(panels, item):
        block, p_i, p_j, p_k, live = item
        upper = factor_two[p_j].reshape(BLOCK_EDGE, R)
        lower = factor_three[p_k].reshape(BLOCK_EDGE, R)
        first = jnp.dot(block.reshape(BLOCK_EDGE * BLOCK_EDGE, BLOCK_EDGE), lower, preferred_element_type=jnp.float32).astype(jnp.bfloat16)
        first = first.reshape(BLOCK_EDGE, BLOCK_EDGE, R).astype(jnp.float32)
        second = jnp.einsum('ajs,jr->ars', first, upper.astype(jnp.float32))
        contrib = second.reshape(BLOCK_EDGE, R * R) * live
        start = (p_i * BLOCK_EDGE).astype(jnp.int32)
        older = lax.dynamic_slice_in_dim(panels, start, BLOCK_EDGE, 0)
        panels = lax.dynamic_update_slice_in_dim(panels, older + contrib, start, 0)
        return (panels, None)
    panels0 = jnp.zeros((NRB * BLOCK_EDGE, R * R), jnp.float32)
    panels, _ = lax.scan(advance, panels0, (blocks, places[0], places[1], places[2], alive))
    panel_b = panels.astype(jnp.bfloat16)
    old_rows = factor_one.reshape(NRB * BLOCK_EDGE, R)
    proj = jnp.dot(panel_b.T, old_rows, preferred_element_type=jnp.float32).astype(jnp.bfloat16)
    rows = jnp.dot(panel_b, proj, preferred_element_type=jnp.float32)
    gmat = jnp.dot(rows.T, rows, precision=lax.Precision.HIGHEST, preferred_element_type=jnp.float32)
    trace_value = jnp.trace(gmat)
    new_rows = (rows * lax.rsqrt(trace_value / (NRB * BLOCK_EDGE * R))).reshape(NRB, BLOCK_EDGE * R)
    gram = gmat * (R / trace_value)
    return (new_rows, gram)
```

```python
import functools

import jax
import jax.numpy as jnp
from jax import lax
from jax.experimental import pallas as pl
from jax.experimental.pallas import tpu as pltpu
from jax.sharding import PartitionSpec as P

F32 = jnp.float32
BF16 = jnp.bfloat16
VMEM = pl.BlockSpec(memory_space=pltpu.VMEM)
SMEM = pl.BlockSpec(memory_space=pltpu.SMEM)
DIRECT_LIMIT = 8


def swap(x, axis, size, mask):
    return lax.ppermute(x, axis, [(i, i ^ mask) for i in range(size)])


def is_direct(size):
    return size <= DIRECT_LIMIT and size & (size - 1) == 0


def params(limit):
    return pltpu.CompilerParams(vmem_limit_bytes=limit)


def dup(u):
    return jnp.concatenate([u, u], axis=1)


def contract_kernel(
    coords, counts, row_place, me, table, block, out, zbuf, vbuf, wbuf, *, slots, row_blocks, edge, rank
):
    s = pl.program_id(0)
    half = edge // 2
    lanes = 2 * rank
    depth = slots * edge
    pos = [row_place[coords[m, s]] for m in range(3)]

    def factor_rows(p):
        piece = (p // row_blocks) ^ me[0]
        at = (piece * row_blocks + p % row_blocks) * edge
        return table[pl.ds(pl.multiple_of(at, edge), edge), :]

    u2 = dup(factor_rows(pos[1])[:, :rank].astype(F32))
    u3 = dup(factor_rows(pos[2])[:, rank:].astype(F32))
    lane = lax.broadcasted_iota(jnp.int32, (edge, lanes), 1)
    low = lane < rank
    low3 = jnp.where(low, u3, 0.0).astype(BF16)
    high3 = jnp.where(low, 0.0, u3).astype(BF16)
    none = jnp.zeros_like(low3)
    weight = jnp.concatenate(
        [
            jnp.concatenate([low3, none], axis=1),
            jnp.concatenate([none, low3], axis=1),
            jnp.concatenate([high3, none], axis=1),
            jnp.concatenate([none, high3], axis=1),
        ],
        axis=0,
    )
    slabs = []
    for j in range(half):
        cols = slice(j * 2 * edge, (j + 1) * 2 * edge)
        slabs.append(jnp.concatenate([block[0, :half, cols], block[0, half:, cols]], axis=1))
    first = jnp.dot(jnp.concatenate(slabs, axis=0), weight, preferred_element_type=F32)
    for j in range(half):
        for q in range(2):
            zbuf[pl.ds(s * edge + 2 * j + q, half, stride=depth), :] = first[
                j * half : (j + 1) * half, q * lanes : (q + 1) * lanes
            ]
    mine = jnp.where(s < counts[0], pos[0] % row_blocks, row_blocks)
    for p in range(row_blocks // 2):
        keep = 2 * p + lane // rank == mine
        wbuf[pl.ds(pl.multiple_of(s * edge, edge), edge), p * lanes : (p + 1) * lanes] = jnp.where(
            keep, u2, 0.0
        )

    @pl.when(s == slots - 1)
    def _():
        left = wbuf[...].T.astype(BF16)
        rows = row_blocks * rank
        for a in range(0, half, 2):
            right = jnp.concatenate(
                [zbuf[a * depth : (a + 1) * depth, :], zbuf[(a + 1) * depth : (a + 2) * depth, :]], axis=1
            ).astype(BF16)
            panel = jnp.dot(left, right, preferred_element_type=F32)
            for b in range(2):
                vbuf[pl.ds(a + b, rows, stride=half), :] = panel[:, b * lanes : (b + 1) * lanes]
        share = rank // out.shape[0]
        for p in range(row_blocks):
            for r in range(rank):
                at = (p * rank + r) * half
                out[r // share, p * half : (p + 1) * half, (r % share) * lanes : (r % share + 1) * lanes] = (
                    vbuf[at : at + half, :].astype(BF16)
                )


def contract(coords, counts, row_place, me, table, blocks, row_blocks, rank, shares):
    slots, edge, width = blocks.shape
    half, lanes = edge // 2, 2 * rank
    out = (shares, row_blocks * half, rank // shares * lanes)
    flops = 2 * slots * edge * width * 4 * edge + 2 * row_blocks * rank * slots * edge * edge * rank
    return pl.pallas_call(
        functools.partial(contract_kernel, slots=slots, row_blocks=row_blocks, edge=edge, rank=rank),
        grid=(slots,),
        in_specs=[SMEM, SMEM, SMEM, SMEM, VMEM, pl.BlockSpec((1, edge, width), lambda s: (s, 0, 0))],
        out_specs=VMEM,
        out_shape=jax.ShapeDtypeStruct(out, BF16),
        scratch_shapes=[
            pltpu.VMEM((half * slots * edge, lanes), F32),
            pltpu.VMEM((row_blocks * rank * half, lanes), F32),
            pltpu.VMEM((slots * edge, row_blocks * rank), F32),
        ],
        compiler_params=params(48 * 1024 * 1024),
        cost_estimate=pl.CostEstimate(
            flops=flops, bytes_accessed=2 * blocks.size + 4 * row_blocks * edge * rank * rank, transcendentals=0
        ),
        name="contract",
    )(coords, counts, row_place, me, table, blocks)


def project_kernel(core, old, *refs, rank, row_blocks):
    pieces, panel, keep, send, buf = refs[:-4], refs[-4], refs[-3], refs[-2], refs[-1]
    total = pieces[0][...].astype(F32)
    for piece in pieces[1:]:
        total = total + piece[...].astype(F32)
    total = total.astype(BF16)
    panel[...] = total
    edge = old.shape[0] // row_blocks
    half, lanes = edge // 2, 2 * rank
    parts = []
    for q in range(2):
        rows = [old[p * edge + q * half : p * edge + (q + 1) * half, :] for p in range(row_blocks)]
        parts.append(jnp.concatenate(rows, axis=0))
    left = jnp.concatenate(parts, axis=1).astype(F32).T.astype(BF16)
    both = jnp.dot(left, total, preferred_element_type=F32)
    low = lax.broadcasted_iota(jnp.int32, (rank, lanes), 1) < rank
    sums = []
    for r in range(total.shape[1] // lanes):
        cols = slice(r * lanes, (r + 1) * lanes)
        own = jnp.where(low, both[:rank, cols], both[rank:, cols])
        sums.append(own + pltpu.roll(own, rank, 1))
    for r in range(0, len(sums), 2):
        buf[:, r // 2 * lanes : (r // 2 + 1) * lanes] = jnp.where(low, sums[r], sums[r + 1])
    count = keep.shape[0]
    if count == rank:
        keep[...] = buf[...].astype(BF16)
        send[...] = jnp.zeros_like(send)
    else:
        keep[...] = buf[pl.ds(pl.multiple_of(core[0] * count, count), count), :].astype(BF16)
        send[...] = buf[pl.ds(pl.multiple_of((1 - core[0]) * count, count), count), :].astype(BF16)


def project(core, old, pieces, rank, row_blocks, halves):
    height, width = pieces[0].shape
    count = rank // halves
    shapes = [
        jax.ShapeDtypeStruct((height, width), BF16),
        jax.ShapeDtypeStruct((count, width // 2), BF16),
        jax.ShapeDtypeStruct((count, width // 2), BF16),
    ]
    return pl.pallas_call(
        functools.partial(project_kernel, rank=rank, row_blocks=row_blocks),
        in_specs=[SMEM] + [VMEM] * (1 + len(pieces)),
        out_specs=[VMEM] * 3,
        out_shape=shapes,
        scratch_shapes=[pltpu.VMEM((rank, width // 2), F32)],
        compiler_params=params(32 * 1024 * 1024),
        name="project",
    )(core, old, *pieces)


def rows_kernel(core, panel, own, other, out, buf, *, rank):
    lanes = 2 * rank
    if own.shape[0] == rank:
        buf[...] = own[...].astype(F32)
    else:
        count = own.shape[0]
        buf[pl.ds(pl.multiple_of(core[0] * count, count), count), :] = own[...].astype(F32)
        buf[pl.ds(pl.multiple_of((1 - core[0]) * count, count), count), :] = other[...].astype(F32)
    low = lax.broadcasted_iota(jnp.int32, (rank, lanes), 1) < rank
    upper, lower = [], []
    for r in range(buf.shape[1] // lanes):
        value = buf[:, r * lanes : (r + 1) * lanes]
        turned = pltpu.roll(value, rank, 1)
        zero = jnp.zeros_like(value)
        upper += [jnp.where(low, value, zero).astype(BF16), jnp.where(low, turned, zero).astype(BF16)]
        lower += [jnp.where(low, zero, turned).astype(BF16), jnp.where(low, zero, value).astype(BF16)]
    right = jnp.concatenate([jnp.concatenate(upper, axis=1), jnp.concatenate(lower, axis=1)], axis=0)
    out[...] = lax.dot_general(
        panel[...], right, (((1,), (1,)), ((), ())), preferred_element_type=F32
    ).astype(BF16)


def row_terms(core, panel, own, other, rank):
    return pl.pallas_call(
        functools.partial(rows_kernel, rank=rank),
        in_specs=[SMEM] + [VMEM] * 3,
        out_specs=VMEM,
        out_shape=jax.ShapeDtypeStruct((panel.shape[0], 2 * rank), BF16),
        scratch_shapes=[pltpu.VMEM((rank, panel.shape[1] // 2), F32)],
        compiler_params=params(32 * 1024 * 1024),
        name="row_terms",
    )(core, panel, own, other)


def gram_kernel(*refs, rank):
    pieces, rows, gram = refs[:-2], refs[-2], refs[-1]
    total = pieces[0][...].astype(F32)
    for piece in pieces[1:]:
        total = total + piece[...].astype(F32)
    rows[...] = total
    full = jnp.dot(total.T, total, precision=lax.Precision.HIGHEST, preferred_element_type=F32)
    gram[...] = full[:rank, :rank] + full[rank:, rank:]


def gram_terms(pieces, rank):
    shapes = [jax.ShapeDtypeStruct(pieces[0].shape, F32), jax.ShapeDtypeStruct((rank, rank), F32)]
    return pl.pallas_call(
        functools.partial(gram_kernel, rank=rank),
        in_specs=[VMEM] * len(pieces),
        out_specs=[VMEM] * 2,
        out_shape=shapes,
        compiler_params=params(32 * 1024 * 1024),
        name="gram_terms",
    )(*pieces)


def body(blocks, coords, counts, row_place, factor_one, factor_two, factor_three):
    edge = blocks.shape[1]
    rank = factor_one.shape[1] // edge
    row_blocks = factor_one.shape[0]
    half = edge // 2
    n_grp, n_dev = lax.axis_size("grp"), lax.axis_size("dev")
    direct = is_direct(n_dev)
    index = lax.axis_index("dev").astype(jnp.int32)
    core = (index % 2).reshape(1)

    packed = jnp.concatenate(
        [f.reshape(row_blocks * edge, rank) for f in (factor_two, factor_three)], axis=1
    )
    if direct:
        same = [packed] + [swap(packed, "dev", n_dev, m) for m in range(2, n_dev, 2)]
        same = jnp.stack(same)
        table = jnp.stack([same, swap(same, "dev", n_dev, 1)], axis=1)
        table = table.reshape(n_dev * row_blocks * edge, 2 * rank)
        me = index.reshape(1)
    else:
        table = lax.all_gather(packed, "dev", axis=0, tiled=True)
        me = jnp.zeros_like(core)

    shares = contract(coords, counts, row_place, me, table, blocks, row_blocks, rank, n_grp)
    if is_direct(n_grp):
        group = lax.axis_index("grp")
        pieces = [lax.dynamic_index_in_dim(shares, group, 0, keepdims=False)]
        for m in range(1, n_grp):
            part = lax.dynamic_index_in_dim(shares, group ^ m, 0, keepdims=False)
            pieces.append(swap(part, "grp", n_grp, m))
    else:
        got = lax.all_to_all(shares, "grp", 0, 0)
        pieces = [got[g] for g in range(n_grp)]

    old = factor_one.reshape(row_blocks * edge, rank)
    panel, keep, send = project(core, old, pieces, rank, row_blocks, 2 if direct else 1)
    if direct:
        chip = (keep.astype(F32) + swap(send, "dev", n_dev, 1).astype(F32)).astype(BF16)
        total = chip.astype(F32)
        for m in range(2, n_dev, 2):
            total = total + swap(chip, "dev", n_dev, m).astype(F32)
        own = total.astype(BF16)
        other = swap(own, "dev", n_dev, 1)
    else:
        own = lax.psum(keep.astype(F32), "dev").astype(BF16)
        other = send
    terms = row_terms(core, panel, own, other, rank)
    if is_direct(n_grp):
        parts = [terms] + [swap(terms, "grp", n_grp, m) for m in range(1, n_grp)]
    else:
        got = lax.all_gather(terms, "grp")
        parts = [got[g] for g in range(n_grp)]
    rows, gram_local = gram_terms(parts, rank)
    if direct:
        chip = gram_local + swap(gram_local, "dev", n_dev, 1)
        gmat = chip
        for m in range(2, n_dev, 2):
            gmat = gmat + swap(chip, "dev", n_dev, m)
    else:
        gmat = lax.psum(gram_local, "dev")
    trace_value = jnp.trace(gmat)
    rows = rows.reshape(row_blocks, half, 2, rank).transpose(0, 2, 1, 3).reshape(row_blocks, edge * rank)
    rows_total = row_blocks * edge * n_dev
    new_rows = rows * lax.rsqrt(trace_value / (rows_total * rank))
    gram = gmat * (rank / trace_value)
    return (new_rows, gram)


def solution(mesh):
    placed = (
        P(("grp", "dev"), None, None),
        P(None, ("grp", "dev")),
        P(("grp", "dev")),
        P(),
        P("dev", None),
        P("dev", None),
        P("dev", None),
    )
    return jax.shard_map(
        body, mesh=mesh, in_specs=placed, out_specs=(P("dev", None), P()), check_vma=False
    )
```

```python
import functools

import jax
import jax.numpy as jnp
from jax import lax
from jax.experimental import pallas as pl
from jax.experimental.pallas import tpu as pltpu
from jax.sharding import PartitionSpec as P

F32 = jnp.float32
BF16 = jnp.bfloat16
VMEM = pl.BlockSpec(memory_space=pltpu.VMEM)
SMEM = pl.BlockSpec(memory_space=pltpu.SMEM)
DIRECT_LIMIT = 8


def partner(i, mask, size):
    return i ^ mask if size & (size - 1) == 0 else (i + mask) % size


def swap(x, axis, size, mask):
    return lax.ppermute(x, axis, [(i, partner(i, mask, size)) for i in range(size)])


def is_direct(size):
    return size <= DIRECT_LIMIT and size & (size - 1) == 0


def params(limit):
    return pltpu.CompilerParams(vmem_limit_bytes=limit)


def dup(u):
    return jnp.concatenate([u, u], axis=1)


def contract_kernel(*refs, n_tables, n_grp, split, slots, row_blocks, edge, rank):
    places, counts, blocks = refs[:3]
    tables, refs = refs[3 : 3 + n_tables], refs[3 + n_tables :]
    outs, refs = refs[: n_grp * split], refs[n_grp * split :]
    place, live, xbuf, fbuf, zbuf, vbuf, wbuf, meta_sem, block_sem = refs
    half = edge // 2
    lanes = 2 * rank
    tile = 8

    meta = [
        pltpu.make_async_copy(source, target, meta_sem.at[i])
        for i, (source, target) in enumerate(((places, place), (counts, live)))
    ]
    loads = [pltpu.make_async_copy(blocks.at[s], xbuf.at[s], block_sem.at[s]) for s in range(slots)]
    for copy in meta + loads:
        copy.start()

    height = tables[0].shape[0]
    total = height * n_tables
    low = lax.broadcasted_iota(jnp.int32, (height, lanes), 1) < rank
    for i in range(n_tables):
        for j in range(half):
            pair = tables[i][:, j * lanes : (j + 1) * lanes].astype(F32)
            turned = pltpu.roll(pair, rank, 1)
            for q in range(2):
                k = 2 * j + q
                at = k // tile * total * tile + i * height * tile + k % tile
                fbuf[pl.ds(at, height, stride=tile), :] = (
                    jnp.where(low, turned, pair) if q else jnp.where(low, pair, turned)
                )
    for copy in meta:
        copy.wait()
    me = lax.axis_index("dev").astype(jnp.int32) if split > 1 else 0
    core = me % split
    per_owner = 2 * row_blocks
    per_core = total // per_owner // split

    def factor_rows(p, which):
        owner = (p // row_blocks) ^ me
        row = (owner % split * per_core + owner // split) * per_owner + which * row_blocks + p % row_blocks
        parts = []
        for k in range(edge // tile):
            at = pl.multiple_of((k * total + row) * tile, tile)
            parts.append(fbuf[pl.ds(at, tile), :])
        return jnp.concatenate(parts, axis=0)

    lane = lax.broadcasted_iota(jnp.int32, (edge, lanes), 1)
    low = lane < rank
    weights = []
    for s in range(slots):
        pos = [place[m, s] for m in range(3)]
        u2 = factor_rows(pos[1], 0)
        u3 = factor_rows(pos[2], 1)
        low3 = jnp.where(low, u3, 0.0).astype(BF16)
        high3 = jnp.where(low, 0.0, u3).astype(BF16)
        none = jnp.zeros_like(low3)
        weights.append(
            jnp.concatenate(
                [
                    jnp.concatenate([low3, none], axis=1),
                    jnp.concatenate([none, low3], axis=1),
                    jnp.concatenate([high3, none], axis=1),
                    jnp.concatenate([none, high3], axis=1),
                ],
                axis=0,
            )
        )
        mine = jnp.where(s < live[0], pos[0] % row_blocks, row_blocks)
        for p in range(row_blocks // 2):
            keep = 2 * p + lane // rank == mine
            wbuf[s * edge : (s + 1) * edge, p * lanes : (p + 1) * lanes] = jnp.where(keep, u2, 0.0)
    left = wbuf[...].T.astype(BF16)

    for s in range(slots):
        loads[s].wait()
        slabs = []
        for j in range(half):
            cols = slice(j * 2 * edge, (j + 1) * 2 * edge)
            slabs.append(jnp.concatenate([xbuf[s, :half, cols], xbuf[s, half:, cols]], axis=1))
        first = jnp.dot(jnp.concatenate(slabs, axis=0), weights[s], preferred_element_type=F32)
        for j in range(half):
            for q in range(2):
                k = 2 * j + q
                at = (s * (edge // tile) + k // tile) * half * tile + k % tile
                zbuf[pl.ds(at, half, stride=tile), :] = first[
                    j * half : (j + 1) * half, q * lanes : (q + 1) * lanes
                ]

    rows = row_blocks * rank
    for a in range(0, half, 2):
        right = jnp.concatenate(
            [
                jnp.concatenate(
                    [
                        zbuf[(k * half + a + b) * tile : (k * half + a + b + 1) * tile, :]
                        for k in range(slots * edge // tile)
                    ],
                    axis=0,
                )
                for b in range(2)
            ],
            axis=1,
        ).astype(BF16)
        panel = jnp.dot(left, right, preferred_element_type=F32)
        for b in range(2):
            at = (a + b) // tile * rows * tile + (a + b) % tile
            vbuf[pl.ds(at, rows, stride=tile), :] = panel[:, b * lanes : (b + 1) * lanes]
    share = rank // (n_grp * split)
    group = lax.axis_index("grp").astype(jnp.int32)
    for i, out in enumerate(outs):
        side, m = divmod(i, n_grp)
        start = (partner(group, m, n_grp) * split + (core + side) % split) * share
        for p in range(row_blocks):
            for r in range(share):
                parts = []
                for k in range(half // tile):
                    at = pl.multiple_of((k * rows + p * rank + r + start) * tile, tile)
                    parts.append(vbuf[pl.ds(at, tile), :])
                out[p * half : (p + 1) * half, r * lanes : (r + 1) * lanes] = jnp.concatenate(
                    parts, axis=0
                ).astype(BF16)


def contract(places, counts, blocks, tables, n_grp, split, row_blocks, rank):
    slots, edge, width = blocks.shape
    half, lanes = edge // 2, 2 * rank
    out = jax.ShapeDtypeStruct((row_blocks * half, rank // (n_grp * split) * lanes), BF16)
    factor_rows = sum(table.shape[0] for table in tables)
    flops = 2 * slots * edge * width * 4 * edge + 2 * row_blocks * rank * slots * edge * edge * rank
    floats = [
        (edge * factor_rows, lanes),
        (slots * edge * half, lanes),
        (row_blocks * rank * half, lanes),
        (slots * edge, row_blocks * rank),
    ]
    held = 2 * blocks.size + sum(4 * rows * columns for rows, columns in floats)
    far = pl.BlockSpec(memory_space=pltpu.HBM)
    return pl.pallas_call(
        functools.partial(
            contract_kernel,
            n_tables=len(tables),
            n_grp=n_grp,
            split=split,
            slots=slots,
            row_blocks=row_blocks,
            edge=edge,
            rank=rank,
        ),
        in_specs=[far] * 3 + [VMEM] * len(tables),
        out_specs=[VMEM] * (n_grp * split),
        out_shape=[out] * (n_grp * split),
        scratch_shapes=[
            pltpu.SMEM(places.shape, jnp.int32),
            pltpu.SMEM(counts.shape, jnp.int32),
            pltpu.VMEM(blocks.shape, BF16),
            *(pltpu.VMEM(shape, F32) for shape in floats),
            pltpu.SemaphoreType.DMA((2,)),
            pltpu.SemaphoreType.DMA((slots,)),
        ],
        compiler_params=params(max(held + 8 * 1024 * 1024, 50 * 1024 * 1024)),
        cost_estimate=pl.CostEstimate(
            flops=flops, bytes_accessed=2 * blocks.size + 4 * row_blocks * edge * rank * rank, transcendentals=0
        ),
        name="contract",
    )(places, counts, blocks, *tables)


def project_kernel(*refs, sides, rank, row_blocks):
    olds, pieces, panel, out = refs[:sides], refs[sides:-2], refs[-2], refs[-1]
    count = len(pieces) // sides
    edge = olds[0].shape[0] // row_blocks
    half, lanes = edge // 2, 2 * rank
    totals, lefts = [], []
    for d in range(sides):
        total = pieces[d * count][...].astype(F32)
        for piece in pieces[d * count + 1 : (d + 1) * count]:
            total = total + piece[...].astype(F32)
        totals.append(total.astype(BF16))
        parts = []
        for q in range(2):
            rows = [olds[d][p * edge + q * half : p * edge + (q + 1) * half, :] for p in range(row_blocks)]
            parts.append(jnp.concatenate(rows, axis=0))
        lefts.append(jnp.concatenate(parts, axis=1))
    total = jnp.concatenate(totals, axis=0)
    panel[...] = total
    left = jnp.concatenate(lefts, axis=0).astype(F32).T.astype(BF16)
    both = jnp.dot(left, total, preferred_element_type=F32)
    low = lax.broadcasted_iota(jnp.int32, (rank, lanes), 1) < rank
    sums = []
    for r in range(total.shape[1] // lanes):
        cols = slice(r * lanes, (r + 1) * lanes)
        own = jnp.where(low, both[:rank, cols], both[rank:, cols])
        sums.append(own + pltpu.roll(own, rank, 1))
    for r in range(0, len(sums), 2):
        out[:, r // 2 * lanes : (r // 2 + 1) * lanes] = jnp.where(low, sums[r], sums[r + 1]).astype(out.dtype)


def project(olds, pieces, rank, row_blocks, kind):
    sides = len(olds)
    height, width = pieces[0].shape
    shapes = [
        jax.ShapeDtypeStruct((height * sides, width), BF16),
        jax.ShapeDtypeStruct((rank, width // 2), kind),
    ]
    return pl.pallas_call(
        functools.partial(project_kernel, sides=sides, rank=rank, row_blocks=row_blocks),
        in_specs=[VMEM] * (sides + len(pieces)),
        out_specs=[VMEM] * 2,
        out_shape=shapes,
        compiler_params=params(24 * 1024 * 1024),
        name="project",
    )(*olds, *pieces)


def rows_kernel(panel, *refs, rank):
    pieces, out = refs[:-1], refs[-1]
    lanes = 2 * rank
    total = pieces[0][...].astype(F32)
    for piece in pieces[1:]:
        total = total + piece[...].astype(F32)
    low = lax.broadcasted_iota(jnp.int32, (rank, lanes), 1) < rank
    zero = jnp.zeros((rank, lanes), F32)
    upper, lower = [], []
    for r in range(total.shape[1] // lanes):
        value = total[:, r * lanes : (r + 1) * lanes]
        turned = pltpu.roll(value, rank, 1)
        upper += [jnp.where(low, value, zero).astype(BF16), jnp.where(low, turned, zero).astype(BF16)]
        lower += [jnp.where(low, zero, turned).astype(BF16), jnp.where(low, zero, value).astype(BF16)]
    right = jnp.concatenate([jnp.concatenate(upper, axis=1), jnp.concatenate(lower, axis=1)], axis=0)
    out[...] = lax.dot_general(
        panel[...], right, (((1,), (1,)), ((), ())), preferred_element_type=F32
    ).astype(BF16)


def row_terms(panel, pieces, rank):
    return pl.pallas_call(
        functools.partial(rows_kernel, rank=rank),
        in_specs=[VMEM] * (1 + len(pieces)),
        out_specs=VMEM,
        out_shape=jax.ShapeDtypeStruct((panel.shape[0], 2 * rank), BF16),
        compiler_params=params(24 * 1024 * 1024),
        name="row_terms",
    )(panel, *pieces)


def gram_kernel(*refs, rank):
    terms, rows, gram = refs[:-2], refs[-2], refs[-1]
    height = rows.shape[0]
    if len(terms) == 1:
        total = terms[0][...]
    else:
        own = terms[0][:height, :] + terms[1][height:, :]
        total = jnp.concatenate([own, terms[0][height:, :] + terms[1][:height, :]], axis=0)
    rows[...] = total[:height, :]
    full = jnp.dot(total.T, total, precision=lax.Precision.HIGHEST, preferred_element_type=F32)
    gram[...] = full[:rank, :rank] + full[rank:, rank:]


def gram_terms(terms, rank):
    height, lanes = terms[0].shape
    shapes = [
        jax.ShapeDtypeStruct((height // len(terms), lanes), F32),
        jax.ShapeDtypeStruct((rank, rank), F32),
    ]
    return pl.pallas_call(
        functools.partial(gram_kernel, rank=rank),
        in_specs=[VMEM] * len(terms),
        out_specs=[VMEM] * 2,
        out_shape=shapes,
        compiler_params=params(24 * 1024 * 1024),
        name="gram_terms",
    )(*terms)


def finish_kernel(*refs, rows_total):
    pieces, rows, new_rows, gram = refs[:-3], refs[-3], refs[-2], refs[-1]
    total = pieces[0][...]
    for piece in pieces[1:]:
        total = total + piece[...]
    rank = total.shape[0]
    square = total.shape
    diagonal = lax.broadcasted_iota(jnp.int32, square, 0) == lax.broadcasted_iota(jnp.int32, square, 1)
    trace = jnp.sum(jnp.where(diagonal, total, 0.0), axis=1, keepdims=True)
    trace = jnp.sum(trace, axis=0, keepdims=True)
    gram[...] = total * (rank / trace)
    scale = lax.rsqrt(trace / (rows_total * rank))
    row_blocks = new_rows.shape[0]
    lanes = 2 * rank
    half = rows.shape[0] // row_blocks
    pairs = half // 2
    low = lax.broadcasted_iota(jnp.int32, (pairs, lanes), 1) < rank
    for p in range(row_blocks):
        even = rows[pl.ds(p * half, pairs, stride=2), :] * scale
        odd = rows[pl.ds(p * half + 1, pairs, stride=2), :] * scale
        lower = jnp.where(low, even, pltpu.roll(odd, rank, 1))
        upper = jnp.where(low, pltpu.roll(even, rank, 1), odd)
        for q, value in enumerate((lower, upper)):
            for i in range(pairs):
                at = (q * pairs + i) * lanes
                new_rows[p : p + 1, at : at + lanes] = value[i : i + 1, :]


def finish(pieces, rows, row_blocks, rows_total):
    rank = pieces[0].shape[0]
    shapes = [
        jax.ShapeDtypeStruct((row_blocks, rows.size // row_blocks), F32),
        jax.ShapeDtypeStruct((rank, rank), F32),
    ]
    return pl.pallas_call(
        functools.partial(finish_kernel, rows_total=rows_total),
        in_specs=[VMEM] * (len(pieces) + 1),
        out_specs=[VMEM] * 2,
        out_shape=shapes,
        compiler_params=params(24 * 1024 * 1024),
        name="finish",
    )(*pieces, rows)


def body(blocks, coords, counts, row_place, factor_one, factor_two, factor_three):
    edge = blocks.shape[1]
    rank = factor_one.shape[1] // edge
    row_blocks = factor_one.shape[0]
    n_grp, n_dev = lax.axis_size("grp"), lax.axis_size("dev")
    direct = is_direct(n_dev)
    split = 2 if direct else 1
    far = range(2, n_dev, 2)

    def sibling(x):
        return swap(x, "dev", n_dev, 1)

    def over_grp(pieces):
        return pieces[:1] + [swap(pieces[m], "grp", n_grp, m) for m in range(1, n_grp)]

    packed = jnp.concatenate([factor_two, factor_three], axis=0)
    if direct:
        tables = [packed] + [swap(packed, "dev", n_dev, m) for m in far]
        tables += [sibling(table) for table in tables]
    else:
        tables = [lax.all_gather(packed, "dev", axis=0, tiled=True)]
    hits = coords[:, :, None] == jnp.arange(row_place.shape[0])[None, None, :]
    places = jnp.sum(jnp.where(hits, row_place[None, None, :], 0), axis=2)
    old = factor_one.reshape(row_blocks * edge, rank)
    olds = [old, sibling(old)] if direct else [old]
    shares = list(contract(places, counts, blocks, tables, n_grp, split, row_blocks, rank))
    pieces = over_grp(shares[:n_grp])
    if direct:
        pieces += over_grp([sibling(share) for share in shares[n_grp:]])

    panel, proj = project(olds, pieces, rank, row_blocks, BF16 if direct else F32)
    if direct:
        projs = [proj] + [swap(proj, "dev", n_dev, m) for m in far]
    else:
        projs = [lax.psum(proj, "dev")]
    terms = row_terms(panel, projs, rank)
    rows = sum(part.astype(F32) for part in over_grp([terms] * n_grp))
    rows, gram_local = gram_terms([rows, sibling(rows)] if direct else [rows], rank)
    if direct:
        grams = [gram_local] + [swap(gram_local, "dev", n_dev, m) for m in far]
    else:
        grams = [lax.psum(gram_local, "dev")]
    return tuple(finish(grams, rows, row_blocks, row_blocks * edge * n_dev))


def solution(mesh):
    placed = (
        P(("grp", "dev"), None, None),
        P(None, ("grp", "dev")),
        P(("grp", "dev")),
        P(),
        P("dev", None),
        P("dev", None),
        P("dev", None),
    )
    return jax.shard_map(
        body, mesh=mesh, in_specs=placed, out_specs=(P("dev", None), P()), check_vma=False
    )
```

```python
import functools

import jax
import jax.numpy as jnp
from jax import lax
from jax.experimental import pallas as pl
from jax.experimental.pallas import tpu as pltpu
from jax.sharding import PartitionSpec as P

F32 = jnp.float32
BF16 = jnp.bfloat16
VMEM = pl.BlockSpec(memory_space=pltpu.VMEM)
SMEM = pl.BlockSpec(memory_space=pltpu.SMEM)
DIRECT_LIMIT = 8


def partner(i, mask, size):
    return i ^ mask if size & (size - 1) == 0 else (i + mask) % size


def swap(x, axis, size, mask):
    return lax.ppermute(x, axis, [(i, partner(i, mask, size)) for i in range(size)])


def is_direct(size):
    return size <= DIRECT_LIMIT and size & (size - 1) == 0


def params(limit):
    return pltpu.CompilerParams(vmem_limit_bytes=limit)


def dup(u):
    return jnp.concatenate([u, u], axis=1)


def contract_kernel(*refs, n_tables, n_grp, split, n_outs, slots, row_blocks, edge, rank):
    places, counts, blocks = refs[:3]
    tables, refs = refs[3 : 3 + n_tables], refs[3 + n_tables :]
    outs, refs = refs[:n_outs], refs[n_outs:]
    place, live, xbuf, fbuf, zbuf, vbuf, wbuf, meta_sem, block_sem = refs
    half = edge // 2
    lanes = 2 * rank
    tile = 8

    meta = [
        pltpu.make_async_copy(source, target, meta_sem.at[i])
        for i, (source, target) in enumerate(((places, place), (counts, live)))
    ]
    loads = [pltpu.make_async_copy(blocks.at[s], xbuf.at[s], block_sem.at[s]) for s in range(slots)]
    for copy in meta + loads:
        copy.start()

    height = tables[0].shape[0]
    total = height * n_tables
    low = lax.broadcasted_iota(jnp.int32, (height, lanes), 1) < rank
    for i in range(n_tables):
        for j in range(half):
            pair = tables[i][:, j * lanes : (j + 1) * lanes].astype(F32)
            turned = pltpu.roll(pair, rank, 1)
            for q in range(2):
                k = 2 * j + q
                at = k // tile * total * tile + i * height * tile + k % tile
                fbuf[pl.ds(at, height, stride=tile), :] = (
                    jnp.where(low, turned, pair) if q else jnp.where(low, pair, turned)
                )
    for copy in meta:
        copy.wait()
    me = lax.axis_index("dev").astype(jnp.int32) if split > 1 else 0
    core = me % split
    per_owner = 2 * row_blocks
    per_core = total // per_owner // split

    def factor_rows(p, which):
        owner = (p // row_blocks) ^ me
        turn = (per_core - owner // split) % per_core if split > 1 else owner
        row = (owner % split * per_core + turn) * per_owner + which * row_blocks + p % row_blocks
        parts = []
        for k in range(edge // tile):
            at = pl.multiple_of((k * total + row) * tile, tile)
            parts.append(fbuf[pl.ds(at, tile), :])
        return jnp.concatenate(parts, axis=0)

    lane = lax.broadcasted_iota(jnp.int32, (edge, lanes), 1)
    low = lane < rank
    weights = []
    for s in range(slots):
        pos = [place[m, s] for m in range(3)]
        u2 = factor_rows(pos[1], 0)
        u3 = factor_rows(pos[2], 1)
        low3 = jnp.where(low, u3, 0.0).astype(BF16)
        high3 = jnp.where(low, 0.0, u3).astype(BF16)
        none = jnp.zeros_like(low3)
        weights.append(
            jnp.concatenate(
                [
                    jnp.concatenate([low3, none], axis=1),
                    jnp.concatenate([none, low3], axis=1),
                    jnp.concatenate([high3, none], axis=1),
                    jnp.concatenate([none, high3], axis=1),
                ],
                axis=0,
            )
        )
        mine = jnp.where(s < live[0], pos[0] % row_blocks, row_blocks)
        for p in range(row_blocks // 2):
            keep = 2 * p + lane // rank == mine
            wbuf[s * edge : (s + 1) * edge, p * lanes : (p + 1) * lanes] = jnp.where(keep, u2, 0.0)
    left = wbuf[...].T.astype(BF16)

    for s in range(slots):
        loads[s].wait()
        slabs = []
        for j in range(half):
            cols = slice(j * 2 * edge, (j + 1) * 2 * edge)
            slabs.append(jnp.concatenate([xbuf[s, :half, cols], xbuf[s, half:, cols]], axis=1))
        first = jnp.dot(jnp.concatenate(slabs, axis=0), weights[s], preferred_element_type=F32)
        for j in range(half):
            for q in range(2):
                k = 2 * j + q
                at = (s * (edge // tile) + k // tile) * half * tile + k % tile
                zbuf[pl.ds(at, half, stride=tile), :] = first[
                    j * half : (j + 1) * half, q * lanes : (q + 1) * lanes
                ]

    rows = row_blocks * rank
    for a in range(0, half, 2):
        right = jnp.concatenate(
            [
                jnp.concatenate(
                    [
                        zbuf[(k * half + a + b) * tile : (k * half + a + b + 1) * tile, :]
                        for k in range(slots * edge // tile)
                    ],
                    axis=0,
                )
                for b in range(2)
            ],
            axis=1,
        ).astype(BF16)
        panel = jnp.dot(left, right, preferred_element_type=F32)
        for b in range(2):
            at = (a + b) // tile * rows * tile + (a + b) % tile
            vbuf[pl.ds(at, rows, stride=tile), :] = panel[:, b * lanes : (b + 1) * lanes]
    share = rank // (n_grp * split)
    group = lax.axis_index("grp").astype(jnp.int32)
    for out, pieces in zip(outs, reduce_layout(n_grp, split, core)):
        for n, (m, h) in enumerate(pieces):
            start = (partner(group, m, n_grp) * split + h) * share
            for p in range(row_blocks):
                for r in range(share):
                    parts = []
                    for k in range(half // tile):
                        at = pl.multiple_of((k * rows + p * rank + r + start) * tile, tile)
                        parts.append(vbuf[pl.ds(at, tile), :])
                    cols = slice((n * share + r) * lanes, (n * share + r + 1) * lanes)
                    out[p * half : (p + 1) * half, cols] = jnp.concatenate(parts, axis=0).astype(BF16)


def contract(places, counts, blocks, tables, n_grp, split, row_blocks, rank):
    slots, edge, width = blocks.shape
    half, lanes = edge // 2, 2 * rank
    part = rank // (n_grp * split) * lanes
    shapes = [
        jax.ShapeDtypeStruct((row_blocks * half, part * len(pieces)), BF16)
        for pieces in reduce_layout(n_grp, split, 0)
    ]
    factor_rows = sum(table.shape[0] for table in tables)
    flops = 2 * slots * edge * width * 4 * edge + 2 * row_blocks * rank * slots * edge * edge * rank
    floats = [
        (edge * factor_rows, lanes),
        (slots * edge * half, lanes),
        (row_blocks * rank * half, lanes),
        (slots * edge, row_blocks * rank),
    ]
    held = 2 * blocks.size + sum(4 * rows * columns for rows, columns in floats)
    far = pl.BlockSpec(memory_space=pltpu.HBM)
    return pl.pallas_call(
        functools.partial(
            contract_kernel,
            n_tables=len(tables),
            n_grp=n_grp,
            split=split,
            n_outs=len(shapes),
            slots=slots,
            row_blocks=row_blocks,
            edge=edge,
            rank=rank,
        ),
        in_specs=[far] * 3 + [VMEM] * len(tables),
        out_specs=[VMEM] * len(shapes),
        out_shape=shapes,
        scratch_shapes=[
            pltpu.SMEM(places.shape, jnp.int32),
            pltpu.SMEM(counts.shape, jnp.int32),
            pltpu.VMEM(blocks.shape, BF16),
            *(pltpu.VMEM(shape, F32) for shape in floats),
            pltpu.SemaphoreType.DMA((2,)),
            pltpu.SemaphoreType.DMA((slots,)),
        ],
        compiler_params=params(max(held + 8 * 1024 * 1024, 50 * 1024 * 1024)),
        cost_estimate=pl.CostEstimate(
            flops=flops, bytes_accessed=2 * blocks.size + 4 * row_blocks * edge * rank * rank, transcendentals=0
        ),
        name="contract",
    )(places, counts, blocks, *tables)


def project_kernel(*refs, sides, rank):
    olds, pieces, panel, out = refs[:sides], refs[sides:-2], refs[-2], refs[-1]
    count = len(pieces) // sides
    width = panel.shape[1]
    lanes = 2 * rank
    totals, lefts = [], []
    for d in range(sides):
        total = pieces[d * count][:, :width].astype(F32)
        for piece in pieces[d * count + 1 : (d + 1) * count]:
            total = total + piece[:, :width].astype(F32)
        totals.append(total.astype(BF16))
        lefts.append(olds[d][:, olds[d].shape[1] - lanes :])
    total = jnp.concatenate(totals, axis=0)
    panel[...] = total
    left = jnp.concatenate(lefts, axis=0).astype(F32).T.astype(BF16)
    both = jnp.dot(left, total, preferred_element_type=F32)
    low = lax.broadcasted_iota(jnp.int32, (rank, lanes), 1) < rank
    sums = []
    for r in range(width // lanes):
        cols = slice(r * lanes, (r + 1) * lanes)
        own = jnp.where(low, both[:rank, cols], both[rank:, cols])
        sums.append(own + pltpu.roll(own, rank, 1))
    for r in range(0, len(sums), 2):
        out[:, r // 2 * lanes : (r // 2 + 1) * lanes] = jnp.where(low, sums[r], sums[r + 1]).astype(out.dtype)


def project(olds, pieces, rank, kind):
    sides = len(olds)
    height, width = pieces[0].shape
    shapes = [
        jax.ShapeDtypeStruct((height * sides, width), BF16),
        jax.ShapeDtypeStruct((rank, width // 2), kind),
    ]
    return pl.pallas_call(
        functools.partial(project_kernel, sides=sides, rank=rank),
        in_specs=[VMEM] * (sides + len(pieces)),
        out_specs=[VMEM] * 2,
        out_shape=shapes,
        compiler_params=params(24 * 1024 * 1024),
        name="project",
    )(*olds, *pieces)


def rows_kernel(panel, *refs, rank):
    pieces, out = refs[:-1], refs[-1]
    lanes = 2 * rank
    total = pieces[0][...].astype(F32)
    for piece in pieces[1:]:
        total = total + piece[...].astype(F32)
    low = lax.broadcasted_iota(jnp.int32, (rank, lanes), 1) < rank
    zero = jnp.zeros((rank, lanes), F32)
    upper, lower = [], []
    for r in range(total.shape[1] // lanes):
        value = total[:, r * lanes : (r + 1) * lanes]
        turned = pltpu.roll(value, rank, 1)
        upper += [jnp.where(low, value, zero).astype(BF16), jnp.where(low, turned, zero).astype(BF16)]
        lower += [jnp.where(low, zero, turned).astype(BF16), jnp.where(low, zero, value).astype(BF16)]
    right = jnp.concatenate([jnp.concatenate(upper, axis=1), jnp.concatenate(lower, axis=1)], axis=0)
    out[...] = lax.dot_general(
        panel[...], right, (((1,), (1,)), ((), ())), preferred_element_type=F32
    ).astype(BF16)


def row_terms(panel, pieces, rank):
    return pl.pallas_call(
        functools.partial(rows_kernel, rank=rank),
        in_specs=[VMEM] * (1 + len(pieces)),
        out_specs=VMEM,
        out_shape=jax.ShapeDtypeStruct((panel.shape[0], 2 * rank), BF16),
        compiler_params=params(24 * 1024 * 1024),
        name="row_terms",
    )(panel, *pieces)


def gram_kernel(*refs, rank):
    terms, rows, gram = refs[:-2], refs[-2], refs[-1]
    height = rows.shape[0]
    if len(terms) == 1:
        total = terms[0][...]
    else:
        own = terms[0][:height, :] + terms[1][height:, :]
        total = jnp.concatenate([own, terms[0][height:, :] + terms[1][:height, :]], axis=0)
    rows[...] = total[:height, :]
    full = jnp.dot(total.T, total, precision=lax.Precision.HIGHEST, preferred_element_type=F32)
    gram[...] = full[:rank, :rank] + full[rank:, rank:]


def gram_terms(terms, rank):
    height, lanes = terms[0].shape
    shapes = [
        jax.ShapeDtypeStruct((height // len(terms), lanes), F32),
        jax.ShapeDtypeStruct((rank, rank), F32),
    ]
    return pl.pallas_call(
        functools.partial(gram_kernel, rank=rank),
        in_specs=[VMEM] * len(terms),
        out_specs=[VMEM] * 2,
        out_shape=shapes,
        compiler_params=params(24 * 1024 * 1024),
        name="gram_terms",
    )(*terms)


def finish_kernel(*refs, rows_total):
    pieces, rows, new_rows, gram = refs[:-3], refs[-3], refs[-2], refs[-1]
    total = pieces[0][...]
    for piece in pieces[1:]:
        total = total + piece[...]
    rank = total.shape[0]
    square = total.shape
    diagonal = lax.broadcasted_iota(jnp.int32, square, 0) == lax.broadcasted_iota(jnp.int32, square, 1)
    trace = jnp.sum(jnp.where(diagonal, total, 0.0), axis=1, keepdims=True)
    trace = jnp.sum(trace, axis=0, keepdims=True)
    gram[...] = total * (rank / trace)
    scale = lax.rsqrt(trace / (rows_total * rank))
    row_blocks = new_rows.shape[0]
    lanes = 2 * rank
    half = rows.shape[0] // row_blocks
    pairs = half // 2
    low = lax.broadcasted_iota(jnp.int32, (pairs, lanes), 1) < rank
    for p in range(row_blocks):
        even = rows[pl.ds(p * half, pairs, stride=2), :] * scale
        odd = rows[pl.ds(p * half + 1, pairs, stride=2), :] * scale
        lower = jnp.where(low, even, pltpu.roll(odd, rank, 1))
        upper = jnp.where(low, pltpu.roll(even, rank, 1), odd)
        for q, value in enumerate((lower, upper)):
            for i in range(pairs):
                at = (q * pairs + i) * lanes
                new_rows[p : p + 1, at : at + lanes] = value[i : i + 1, :]


def finish(pieces, rows, row_blocks, rows_total):
    rank = pieces[0].shape[0]
    shapes = [
        jax.ShapeDtypeStruct((row_blocks, rows.size // row_blocks), F32),
        jax.ShapeDtypeStruct((rank, rank), F32),
    ]
    return pl.pallas_call(
        functools.partial(finish_kernel, rows_total=rows_total),
        in_specs=[VMEM] * (len(pieces) + 1),
        out_specs=[VMEM] * 2,
        out_shape=shapes,
        compiler_params=params(24 * 1024 * 1024),
        name="finish",
    )(*pieces, rows)


def two_step(n_grp, split):
    return n_grp == 4 and split == 2


def reduce_layout(n_grp, split, core):
    if not two_step(n_grp, split):
        return [[(m, h) for h in range(split)] for m in range(n_grp)]
    near, side = 1 + core, 2 - core
    other = 1 - core
    return [
        [(near, core), (3, core)],
        [(side, other), (3, other)],
        [(0, core), (0, other), (side, core), (near, other)],
    ]


def reduce_panel(shares, old, n_grp, n_dev, split):
    if not two_step(n_grp, split):
        width = shares[0].shape[1] // split
        parts = [shares[0]] + [swap(shares[m], "grp", n_grp, m) for m in range(1, n_grp)]
        if split == 1:
            return [old], parts
        core = lax.axis_index("dev") % split

        def side(i):
            at = (core + i) % split * width
            return [lax.dynamic_slice_in_dim(part, at, width, 1) for part in parts]

        total = sum(part.astype(F32) for part in side(1)).astype(BF16)
        crossed = swap(jnp.concatenate([total, old], axis=1), "dev", n_dev, 1)
        own = sum(part.astype(F32) for part in side(0)).astype(BF16)
        return [old, crossed], [own, crossed]

    def send(x, own, cross):
        pairs = []
        for g in range(n_grp):
            for d in range(n_dev):
                core = d % 2
                mask = 1 + core if own else 2 - core
                pairs.append((g * n_dev + d, (g ^ mask) * n_dev + (d ^ cross)))
        return lax.ppermute(x, ("grp", "dev"), pairs)

    width = shares[0].shape[1] // 2
    first = send(shares[0], True, 0).astype(F32)
    second = send(shares[1], False, 0).astype(F32)
    rest = [shares[2][:, i * width : (i + 1) * width].astype(F32) for i in range(4)]
    own = send((rest[2] + first[:, width:]).astype(BF16), False, 0)
    other = send((rest[3] + second[:, width:]).astype(BF16), True, 1)
    crossed = (rest[1] + second[:, :width]).astype(BF16)
    crossed = swap(jnp.concatenate([crossed, old], axis=1), "dev", n_dev, 1)
    kept = (rest[0] + first[:, :width]).astype(BF16)
    return [old, crossed], [kept, own, crossed, other]


def body(blocks, coords, counts, row_place, factor_one, factor_two, factor_three):
    edge = blocks.shape[1]
    rank = factor_one.shape[1] // edge
    row_blocks = factor_one.shape[0]
    n_grp, n_dev = lax.axis_size("grp"), lax.axis_size("dev")
    direct = is_direct(n_dev)
    split = 2 if direct else 1
    far = range(n_dev - 2, 0, -2)

    def sibling(x):
        return swap(x, "dev", n_dev, 1)

    def over_grp(pieces):
        return pieces[:1] + [swap(pieces[m], "grp", n_grp, m) for m in range(n_grp - 1, 0, -1)]

    packed = jnp.concatenate([factor_two, factor_three], axis=0)
    if direct:
        tables = [packed] + [swap(packed, "dev", n_dev, m) for m in far]
        tables += [sibling(table) for table in tables]
    else:
        tables = [lax.all_gather(packed, "dev", axis=0, tiled=True)]
    hits = coords[:, :, None] == jnp.arange(row_place.shape[0])[None, None, :]
    places = jnp.sum(jnp.where(hits, row_place[None, None, :], 0), axis=2)
    shares = list(contract(places, counts, blocks, tables, n_grp, split, row_blocks, rank))
    factor_one, shares[0] = lax.optimization_barrier((factor_one, shares[0]))
    old = factor_one.reshape(row_blocks, 2, edge // 2, rank).transpose(0, 2, 1, 3)
    old = old.reshape(row_blocks * edge // 2, 2 * rank)
    olds, pieces = reduce_panel(shares, old, n_grp, n_dev, split)
    panel, proj = project(olds, pieces, rank, BF16 if direct else F32)
    if direct:
        projs = [proj] + [swap(proj, "dev", n_dev, m) for m in far]
    else:
        projs = [lax.psum(proj, "dev")]
    terms = row_terms(panel, projs, rank)
    rows = sum(part.astype(F32) for part in over_grp([terms] * n_grp))
    rows, gram_local = gram_terms([rows, sibling(rows)] if direct else [rows], rank)
    if direct:
        grams = [gram_local] + [swap(gram_local, "dev", n_dev, m) for m in far]
    else:
        grams = [lax.psum(gram_local, "dev")]
    return tuple(finish(grams, rows, row_blocks, row_blocks * edge * n_dev))


def solution(mesh):
    placed = (
        P(("grp", "dev"), None, None),
        P(None, ("grp", "dev")),
        P(("grp", "dev")),
        P(),
        P("dev", None),
        P("dev", None),
        P("dev", None),
    )
    return jax.shard_map(
        body, mesh=mesh, in_specs=placed, out_specs=(P("dev", None), P()), check_vma=False
    )
```

```python
import functools

import jax
import jax.numpy as jnp
from jax import lax
from jax.experimental import pallas as pl
from jax.experimental.pallas import tpu as pltpu
from jax.sharding import PartitionSpec as P

F32 = jnp.float32
BF16 = jnp.bfloat16
VMEM = pl.BlockSpec(memory_space=pltpu.VMEM)
SMEM = pl.BlockSpec(memory_space=pltpu.SMEM)
DIRECT_LIMIT = 8
GROUPS = (0, 1, 4)


def partner(i, mask, size):
    return i ^ mask if size & (size - 1) == 0 else (i + mask) % size


def swap(x, axis, size, mask):
    return lax.ppermute(x, axis, [(i, partner(i, mask, size)) for i in range(size)])


def is_direct(size):
    return size <= DIRECT_LIMIT and size & (size - 1) == 0


def params(limit):
    return pltpu.CompilerParams(vmem_limit_bytes=limit)


def dup(u):
    return jnp.concatenate([u, u], axis=1)


def contract_kernel(*refs, n_tables, n_grp, split, n_outs, slots, row_blocks, edge, rank):
    places, blocks = refs[:2]
    tables, refs = refs[2 : 2 + n_tables], refs[2 + n_tables :]
    outs, refs = refs[:n_outs], refs[n_outs:]
    place, xbuf, fbuf, zbuf, vbuf, wbuf, meta_sem, block_sem = refs
    half = edge // 2
    lanes = 2 * rank
    tile = 8

    meta = pltpu.make_async_copy(places, place, meta_sem.at[0])
    loads = [pltpu.make_async_copy(blocks.at[s], xbuf.at[s], block_sem.at[s]) for s in range(slots)]
    for copy in [meta] + loads:
        copy.start()

    owners = [table.at[i] for table in tables for i in range(table.shape[0])]
    height = owners[0].shape[0]
    total = height * len(owners)
    low = lax.broadcasted_iota(jnp.int32, (height, lanes), 1) < rank
    for i, owner in enumerate(owners):
        for j in range(half):
            pair = owner[:, j * lanes : (j + 1) * lanes].astype(F32)
            turned = pltpu.roll(pair, rank, 1)
            for q in range(2):
                k = 2 * j + q
                at = k // tile * total * tile + i * height * tile + k % tile
                fbuf[pl.ds(at, height, stride=tile), :] = (
                    jnp.where(low, turned, pair) if q else jnp.where(low, pair, turned)
                )
    meta.wait()
    me = lax.axis_index("dev").astype(jnp.int32) if split > 1 else 0
    core = me % split
    per_owner = 2 * row_blocks
    per_core = total // per_owner // split

    def factor_rows(p, which):
        owner = (p // row_blocks) ^ me
        turn = (per_core - owner // split) % per_core if split > 1 else owner
        row = (owner % split * per_core + turn) * per_owner + which * row_blocks + p % row_blocks
        parts = []
        for k in range(edge // tile):
            at = pl.multiple_of((k * total + row) * tile, tile)
            parts.append(fbuf[pl.ds(at, tile), :])
        return jnp.concatenate(parts, axis=0)

    lane = lax.broadcasted_iota(jnp.int32, (edge, lanes), 1)
    low = lane < rank
    weights = []
    for s in range(slots):
        pos = [place[m, s] for m in range(3)]
        u2 = factor_rows(pos[1], 0)
        u3 = factor_rows(pos[2], 1)
        low3 = jnp.where(low, u3, 0.0).astype(BF16)
        high3 = jnp.where(low, 0.0, u3).astype(BF16)
        none = jnp.zeros_like(low3)
        weights.append(
            jnp.concatenate(
                [
                    jnp.concatenate([low3, none], axis=1),
                    jnp.concatenate([none, low3], axis=1),
                    jnp.concatenate([high3, none], axis=1),
                    jnp.concatenate([none, high3], axis=1),
                ],
                axis=0,
            )
        )
        for p in range(row_blocks // 2):
            keep = 2 * p + lane // rank == pos[0]
            wbuf[s * edge : (s + 1) * edge, p * lanes : (p + 1) * lanes] = jnp.where(keep, u2, 0.0)
    left = wbuf[...].T.astype(BF16)

    for s in range(slots):
        if s in GROUPS:
            last = min([g for g in GROUPS if g > s] + [slots])
            for t in range(s, last):
                loads[t].wait()
        slabs = []
        for j in range(half):
            cols = slice(j * 2 * edge, (j + 1) * 2 * edge)
            slabs.append(jnp.concatenate([xbuf[s, :half, cols], xbuf[s, half:, cols]], axis=1))
        first = jnp.dot(jnp.concatenate(slabs, axis=0), weights[s], preferred_element_type=F32)
        for j in range(half):
            for q in range(2):
                k = 2 * j + q
                at = (s * (edge // tile) + k // tile) * half * tile + k % tile
                zbuf[pl.ds(at, half, stride=tile), :] = first[
                    j * half : (j + 1) * half, q * lanes : (q + 1) * lanes
                ]

    rows = row_blocks * rank
    for a in range(0, half, 2):
        right = jnp.concatenate(
            [
                jnp.concatenate(
                    [
                        zbuf[(k * half + a + b) * tile : (k * half + a + b + 1) * tile, :]
                        for k in range(slots * edge // tile)
                    ],
                    axis=0,
                )
                for b in range(2)
            ],
            axis=1,
        ).astype(BF16)
        panel = jnp.dot(left, right, preferred_element_type=F32)
        for b in range(2):
            at = (a + b) // tile * rows * tile + (a + b) % tile
            vbuf[pl.ds(at, rows, stride=tile), :] = panel[:, b * lanes : (b + 1) * lanes]
    share = rank // (n_grp * split)
    group = lax.axis_index("grp").astype(jnp.int32)
    for out, pieces in zip(outs, reduce_layout(n_grp, split, core)):
        for n, (m, h) in enumerate(pieces):
            start = (partner(group, m, n_grp) * split + h) * share
            for p in range(row_blocks):
                for r in range(share):
                    parts = []
                    for k in range(half // tile):
                        at = pl.multiple_of((k * rows + p * rank + r + start) * tile, tile)
                        parts.append(vbuf[pl.ds(at, tile), :])
                    cols = slice((n * share + r) * lanes, (n * share + r + 1) * lanes)
                    out[p * half : (p + 1) * half, cols] = jnp.concatenate(parts, axis=0).astype(BF16)


def contract(places, blocks, tables, n_grp, split, row_blocks, rank):
    slots, edge, width = blocks.shape
    half, lanes = edge // 2, 2 * rank
    part = rank // (n_grp * split) * lanes
    shapes = [
        jax.ShapeDtypeStruct((row_blocks * half, part * len(pieces)), BF16)
        for pieces in reduce_layout(n_grp, split, 0)
    ]
    factor_rows = sum(table.shape[0] * table.shape[1] for table in tables)
    flops = 2 * slots * edge * width * 4 * edge + 2 * row_blocks * rank * slots * edge * edge * rank
    floats = [
        (edge * factor_rows, lanes),
        (slots * edge * half, lanes),
        (row_blocks * rank * half, lanes),
        (slots * edge, row_blocks * rank),
    ]
    held = 2 * blocks.size + sum(4 * rows * columns for rows, columns in floats)
    far = pl.BlockSpec(memory_space=pltpu.HBM)
    return pl.pallas_call(
        functools.partial(
            contract_kernel,
            n_tables=len(tables),
            n_grp=n_grp,
            split=split,
            n_outs=len(shapes),
            slots=slots,
            row_blocks=row_blocks,
            edge=edge,
            rank=rank,
        ),
        in_specs=[far] * 2 + [VMEM] * len(tables),
        out_specs=[VMEM] * len(shapes),
        out_shape=shapes,
        scratch_shapes=[
            pltpu.SMEM(places.shape, jnp.int32),
            pltpu.VMEM(blocks.shape, BF16),
            *(pltpu.VMEM(shape, F32) for shape in floats),
            pltpu.SemaphoreType.DMA((1,)),
            pltpu.SemaphoreType.DMA((slots,)),
        ],
        compiler_params=params(max(held + 8 * 1024 * 1024, 50 * 1024 * 1024)),
        cost_estimate=pl.CostEstimate(
            flops=flops, bytes_accessed=2 * blocks.size + 4 * row_blocks * edge * rank * rank, transcendentals=0
        ),
        name="contract",
    )(places, blocks, *tables)


def project_kernel(*refs, sides, rank):
    pieces, olds, panel, out = refs[: -sides - 2], refs[-sides - 2 : -2], refs[-2], refs[-1]
    count = len(pieces) // sides
    width = panel.shape[1]
    lanes = 2 * rank
    totals, lefts = [], []
    for d in range(sides):
        total = pieces[d * count][:, :width].astype(F32)
        for piece in pieces[d * count + 1 : (d + 1) * count]:
            total = total + piece[:, :width].astype(F32)
        totals.append(total.astype(BF16))
        lefts.append(olds[d][:, olds[d].shape[1] - lanes :])
    total = jnp.concatenate(totals, axis=0)
    panel[...] = total
    left = jnp.concatenate(lefts, axis=0).astype(F32).T.astype(BF16)
    both = jnp.dot(left, total, preferred_element_type=F32)
    low = lax.broadcasted_iota(jnp.int32, (rank, lanes), 1) < rank
    sums = []
    for r in range(width // lanes):
        cols = slice(r * lanes, (r + 1) * lanes)
        own = jnp.where(low, both[:rank, cols], both[rank:, cols])
        sums.append(own + pltpu.roll(own, rank, 1))
    for r in range(0, len(sums), 2):
        out[:, r // 2 * lanes : (r // 2 + 1) * lanes] = jnp.where(low, sums[r], sums[r + 1]).astype(out.dtype)


def project(olds, pieces, rank, kind):
    sides = len(olds)
    height, width = pieces[0].shape
    shapes = [
        jax.ShapeDtypeStruct((height * sides, width), BF16),
        jax.ShapeDtypeStruct((rank, width // 2), kind),
    ]
    return pl.pallas_call(
        functools.partial(project_kernel, sides=sides, rank=rank),
        in_specs=[VMEM] * (sides + len(pieces)),
        out_specs=[VMEM] * 2,
        out_shape=shapes,
        compiler_params=params(24 * 1024 * 1024),
        name="project",
    )(*pieces, *olds)


def rows_kernel(panel, *refs, rank):
    pieces, out = refs[:-1], refs[-1]
    lanes = 2 * rank
    total = pieces[0][...].astype(F32)
    for piece in pieces[1:]:
        total = total + piece[...].astype(F32)
    low = lax.broadcasted_iota(jnp.int32, (rank, lanes), 1) < rank
    zero = jnp.zeros((rank, lanes), F32)
    upper, lower = [], []
    for r in range(total.shape[1] // lanes):
        value = total[:, r * lanes : (r + 1) * lanes]
        turned = pltpu.roll(value, rank, 1)
        upper += [jnp.where(low, value, zero).astype(BF16), jnp.where(low, turned, zero).astype(BF16)]
        lower += [jnp.where(low, zero, turned).astype(BF16), jnp.where(low, zero, value).astype(BF16)]
    right = jnp.concatenate([jnp.concatenate(upper, axis=1), jnp.concatenate(lower, axis=1)], axis=0)
    out[...] = lax.dot_general(
        panel[...], right, (((1,), (1,)), ((), ())), preferred_element_type=F32
    ).astype(BF16)


def row_terms(panel, pieces, rank):
    return pl.pallas_call(
        functools.partial(rows_kernel, rank=rank),
        in_specs=[VMEM] * (1 + len(pieces)),
        out_specs=VMEM,
        out_shape=jax.ShapeDtypeStruct((panel.shape[0], 2 * rank), BF16),
        compiler_params=params(24 * 1024 * 1024),
        name="row_terms",
    )(panel, *pieces)


def gram_kernel(*refs, rank):
    terms, rows, gram = refs[:-2], refs[-2], refs[-1]
    height = rows.shape[0]
    if len(terms) == 1:
        total = terms[0][...]
    else:
        own = terms[0][:height, :] + terms[1][height:, :]
        total = jnp.concatenate([own, terms[0][height:, :] + terms[1][:height, :]], axis=0)
    rows[...] = total[:height, :]
    full = jnp.dot(total.T, total, precision=lax.Precision.HIGHEST, preferred_element_type=F32)
    square = full[:rank, :rank] + full[rank:, rank:]
    gram[...] = jnp.concatenate([square[: rank // 2, :], square[rank // 2 :, :]], axis=1)


def gram_terms(terms, rank):
    height, lanes = terms[0].shape
    shapes = [
        jax.ShapeDtypeStruct((height // len(terms), lanes), F32),
        jax.ShapeDtypeStruct((rank // 2, lanes), F32),
    ]
    return pl.pallas_call(
        functools.partial(gram_kernel, rank=rank),
        in_specs=[VMEM] * len(terms),
        out_specs=[VMEM] * 2,
        out_shape=shapes,
        compiler_params=params(24 * 1024 * 1024),
        name="gram_terms",
    )(*terms)


def finish_kernel(*refs, rows_total):
    pieces, rows, new_rows, gram = refs[:-3], refs[-3], refs[-2], refs[-1]
    total = pieces[0][...]
    for piece in pieces[1:]:
        total = total + piece[...]
    rank = gram.shape[0]
    total = jnp.concatenate([total[:, :rank], total[:, rank:]], axis=0)
    square = total.shape
    diagonal = lax.broadcasted_iota(jnp.int32, square, 0) == lax.broadcasted_iota(jnp.int32, square, 1)
    trace = jnp.sum(jnp.where(diagonal, total, 0.0), axis=1, keepdims=True)
    trace = jnp.sum(trace, axis=0, keepdims=True)
    gram[...] = total * (rank / trace)
    scale = lax.rsqrt(trace / (rows_total * rank))
    row_blocks = new_rows.shape[0]
    lanes = 2 * rank
    half = rows.shape[0] // row_blocks
    pairs = half // 2
    low = lax.broadcasted_iota(jnp.int32, (pairs, lanes), 1) < rank
    for p in range(row_blocks):
        even = rows[pl.ds(p * half, pairs, stride=2), :] * scale
        odd = rows[pl.ds(p * half + 1, pairs, stride=2), :] * scale
        lower = jnp.where(low, even, pltpu.roll(odd, rank, 1))
        upper = jnp.where(low, pltpu.roll(even, rank, 1), odd)
        for q, value in enumerate((lower, upper)):
            for i in range(pairs):
                at = (q * pairs + i) * lanes
                new_rows[p : p + 1, at : at + lanes] = value[i : i + 1, :]


def finish(pieces, rows, row_blocks, rows_total):
    rank = pieces[0].shape[1] // 2
    shapes = [
        jax.ShapeDtypeStruct((row_blocks, rows.size // row_blocks), F32),
        jax.ShapeDtypeStruct((rank, rank), F32),
    ]
    return pl.pallas_call(
        functools.partial(finish_kernel, rows_total=rows_total),
        in_specs=[VMEM] * (len(pieces) + 1),
        out_specs=[VMEM] * 2,
        out_shape=shapes,
        compiler_params=params(24 * 1024 * 1024),
        name="finish",
    )(*pieces, rows)


def two_step(n_grp, split):
    return n_grp == 4 and split == 2


def reduce_layout(n_grp, split, core):
    if not two_step(n_grp, split):
        return [[(m, h) for h in range(split)] for m in range(n_grp)]
    near, side = 1 + core, 2 - core
    other = 1 - core
    return [
        [(near, core), (3, core)],
        [(side, other), (3, other)],
        [(side, core)],
        [(0, core), (0, other), (near, other)],
    ]


def reduce_panel(shares, old, n_grp, n_dev, split):
    if not two_step(n_grp, split):
        width = shares[0].shape[1] // split
        parts = [shares[0]] + [swap(shares[m], "grp", n_grp, m) for m in range(1, n_grp)]
        if split == 1:
            return [old], parts
        core = lax.axis_index("dev") % split

        def side(i):
            at = (core + i) % split * width
            return [lax.dynamic_slice_in_dim(part, at, width, 1) for part in parts]

        total = sum(part.astype(F32) for part in side(1)).astype(BF16)
        crossed = swap(jnp.concatenate([total, old], axis=1), "dev", n_dev, 1)
        own = sum(part.astype(F32) for part in side(0)).astype(BF16)
        return [old, crossed], [own, crossed]

    def send(x, own, cross):
        pairs = []
        for g in range(n_grp):
            for d in range(n_dev):
                core = d % 2
                mask = 1 + core if own else 2 - core
                pairs.append((g * n_dev + d, (g ^ mask) * n_dev + (d ^ cross)))
        return lax.ppermute(x, ("grp", "dev"), pairs)

    width = shares[0].shape[1] // 2
    first = send(shares[0], True, 0).astype(F32)
    second = send(shares[1], False, 0).astype(F32)
    own = send((shares[2].astype(F32) + first[:, width:]).astype(BF16), False, 0)
    rest = [shares[3][:, i * width : (i + 1) * width].astype(F32) for i in range(3)]
    other = send((rest[2] + second[:, width:]).astype(BF16), True, 1)
    crossed = (rest[1] + second[:, :width]).astype(BF16)
    crossed = swap(jnp.concatenate([crossed, old], axis=1), "dev", n_dev, 1)
    kept = (rest[0] + first[:, :width]).astype(BF16)
    return [old, crossed], [kept, own, other, crossed]


def body(blocks, coords, counts, row_place, factor_one, factor_two, factor_three):
    edge = blocks.shape[1]
    rank = factor_one.shape[1] // edge
    row_blocks = factor_one.shape[0]
    n_grp, n_dev = lax.axis_size("grp"), lax.axis_size("dev")
    direct = is_direct(n_dev)
    split = 2 if direct else 1
    far = range(n_dev - 2, 0, -2)

    def sibling(x):
        return swap(x, "dev", n_dev, 1)

    def over_grp(pieces):
        return pieces[:1] + [swap(pieces[m], "grp", n_grp, m) for m in range(n_grp - 1, 0, -1)]

    packed = jnp.concatenate([factor_two, factor_three], axis=0)
    if direct:
        tables = [jnp.stack([packed] + [swap(packed, "dev", n_dev, m) for m in far])]
        tables.append(sibling(tables[0]))
    else:
        tables = [lax.all_gather(packed, "dev", axis=0)]
    hits = coords[:, :, None] == jnp.arange(row_place.shape[0])[None, None, :]
    places = jnp.sum(jnp.where(hits, row_place[None, None, :], 0), axis=2)
    live = jnp.arange(coords.shape[1])[None, :] < counts[0]
    row = jnp.where(live, places % row_blocks, row_blocks)
    places = jnp.where(jnp.arange(coords.shape[0])[:, None] == 0, row, places)
    shares = list(contract(places, blocks, tables, n_grp, split, row_blocks, rank))
    factor_one, shares[0] = lax.optimization_barrier((factor_one, shares[0]))
    old = factor_one.reshape(row_blocks, 2, edge // 2, rank).transpose(0, 2, 1, 3)
    old = old.reshape(row_blocks * edge // 2, 2 * rank)
    olds, pieces = reduce_panel(shares, old, n_grp, n_dev, split)
    panel, proj = project(olds, pieces, rank, BF16 if direct else F32)
    if direct:
        projs = [proj] + [swap(proj, "dev", n_dev, m) for m in far]
    else:
        projs = [lax.psum(proj, "dev")]
    terms = row_terms(panel, projs, rank)
    rows = sum(part.astype(F32) for part in over_grp([terms] * n_grp))
    rows, gram_local = gram_terms([rows, sibling(rows)] if direct else [rows], rank)
    if direct:
        grams = [gram_local] + [swap(gram_local, "dev", n_dev, m) for m in far]
    else:
        grams = [lax.psum(gram_local, "dev")]
    return tuple(finish(grams, rows, row_blocks, row_blocks * edge * n_dev))


def solution(mesh):
    placed = (
        P(("grp", "dev"), None, None),
        P(None, ("grp", "dev")),
        P(("grp", "dev")),
        P(),
        P("dev", None),
        P("dev", None),
        P("dev", None),
    )
    return jax.shard_map(
        body, mesh=mesh, in_specs=placed, out_specs=(P("dev", None), P()), check_vma=False
    )
```

```python
import functools

import jax
import jax.numpy as jnp
from jax import lax
from jax.experimental import pallas as pl
from jax.experimental.pallas import tpu as pltpu
from jax.sharding import PartitionSpec as P

F32 = jnp.float32
BF16 = jnp.bfloat16
VMEM = pl.BlockSpec(memory_space=pltpu.VMEM)
SMEM = pl.BlockSpec(memory_space=pltpu.SMEM)
DIRECT_LIMIT = 8
GROUPS = (0, 1, 4)


def partner(i, mask, size):
    return i ^ mask if size & (size - 1) == 0 else (i + mask) % size


def swap(x, axis, size, mask):
    return lax.ppermute(x, axis, [(i, partner(i, mask, size)) for i in range(size)])


def far_masks(size):
    masks = list(range(2, size, 2))
    return masks[1:2] + masks[:1] + masks[2:]


def is_direct(size):
    return size <= DIRECT_LIMIT and size & (size - 1) == 0


def params(limit):
    return pltpu.CompilerParams(vmem_limit_bytes=limit)


def dup(u):
    return jnp.concatenate([u, u], axis=1)


def contract_kernel(*refs, n_tables, n_grp, split, n_outs, slots, row_blocks, edge, rank):
    places, blocks = refs[:2]
    tables, refs = refs[2 : 2 + n_tables], refs[2 + n_tables :]
    outs, refs = refs[:n_outs], refs[n_outs:]
    place, xbuf, fbuf, zbuf, vbuf, wbuf, meta_sem, block_sem = refs
    half = edge // 2
    lanes = 2 * rank
    tile = 8

    meta = pltpu.make_async_copy(places, place, meta_sem.at[0])
    loads = [pltpu.make_async_copy(blocks.at[s], xbuf.at[s], block_sem.at[s]) for s in range(slots)]
    for copy in [meta] + loads:
        copy.start()

    owners = [table.at[i] for table in tables for i in range(table.shape[0])]
    height = owners[0].shape[0]
    total = height * len(owners)
    low = lax.broadcasted_iota(jnp.int32, (height, lanes), 1) < rank
    for i, owner in enumerate(owners):
        for j in range(half):
            pair = owner[:, j * lanes : (j + 1) * lanes].astype(F32)
            turned = pltpu.roll(pair, rank, 1)
            for q in range(2):
                k = 2 * j + q
                at = k // tile * total * tile + i * height * tile + k % tile
                fbuf[pl.ds(at, height, stride=tile), :] = (
                    jnp.where(low, turned, pair) if q else jnp.where(low, pair, turned)
                )
    meta.wait()
    me = lax.axis_index("dev").astype(jnp.int32) if split > 1 else 0
    core = me % split
    per_owner = 2 * row_blocks
    per_core = total // per_owner // split

    def factor_rows(p, which):
        owner = (p // row_blocks) ^ me
        turn = owner
        if split > 1:
            turn = sum(jnp.where(owner // 2 == m // 2, i + 1, 0) for i, m in enumerate(far_masks(per_core * 2)))
        row = (owner % split * per_core + turn) * per_owner + which * row_blocks + p % row_blocks
        parts = []
        for k in range(edge // tile):
            at = pl.multiple_of((k * total + row) * tile, tile)
            parts.append(fbuf[pl.ds(at, tile), :])
        return jnp.concatenate(parts, axis=0)

    lane = lax.broadcasted_iota(jnp.int32, (edge, lanes), 1)
    low = lane < rank
    weights = []
    for s in range(slots):
        pos = [place[m, s] for m in range(3)]
        u2 = factor_rows(pos[1], 0)
        u3 = factor_rows(pos[2], 1)
        low3 = jnp.where(low, u3, 0.0).astype(BF16)
        high3 = jnp.where(low, 0.0, u3).astype(BF16)
        none = jnp.zeros_like(low3)
        weights.append(
            jnp.concatenate(
                [
                    jnp.concatenate([low3, none], axis=1),
                    jnp.concatenate([none, low3], axis=1),
                    jnp.concatenate([high3, none], axis=1),
                    jnp.concatenate([none, high3], axis=1),
                ],
                axis=0,
            )
        )
        for p in range(row_blocks // 2):
            keep = 2 * p + lane // rank == pos[0]
            wbuf[s * edge : (s + 1) * edge, p * lanes : (p + 1) * lanes] = jnp.where(keep, u2, 0.0)
    left = wbuf[...].T.astype(BF16)

    for s in range(slots):
        if s in GROUPS:
            last = min([g for g in GROUPS if g > s] + [slots])
            for t in range(s, last):
                loads[t].wait()
        slabs = []
        for j in range(half):
            cols = slice(j * 2 * edge, (j + 1) * 2 * edge)
            slabs.append(jnp.concatenate([xbuf[s, :half, cols], xbuf[s, half:, cols]], axis=1))
        first = jnp.dot(jnp.concatenate(slabs, axis=0), weights[s], preferred_element_type=F32)
        for j in range(half):
            for q in range(2):
                k = 2 * j + q
                at = (s * (edge // tile) + k // tile) * half * tile + k % tile
                zbuf[pl.ds(at, half, stride=tile), :] = first[
                    j * half : (j + 1) * half, q * lanes : (q + 1) * lanes
                ]

    rows = row_blocks * rank
    for a in range(0, half, 2):
        right = jnp.concatenate(
            [
                jnp.concatenate(
                    [
                        zbuf[(k * half + a + b) * tile : (k * half + a + b + 1) * tile, :]
                        for k in range(slots * edge // tile)
                    ],
                    axis=0,
                )
                for b in range(2)
            ],
            axis=1,
        ).astype(BF16)
        panel = jnp.dot(left, right, preferred_element_type=F32)
        for b in range(2):
            at = (a + b) // tile * rows * tile + (a + b) % tile
            vbuf[pl.ds(at, rows, stride=tile), :] = panel[:, b * lanes : (b + 1) * lanes]
    share = rank // (n_grp * split)
    group = lax.axis_index("grp").astype(jnp.int32)
    for out, pieces in zip(outs, reduce_layout(n_grp, split, core)):
        for n, (m, h) in enumerate(pieces):
            start = (partner(group, m, n_grp) * split + h) * share
            for p in range(row_blocks):
                for r in range(share):
                    parts = []
                    for k in range(half // tile):
                        at = pl.multiple_of((k * rows + p * rank + r + start) * tile, tile)
                        parts.append(vbuf[pl.ds(at, tile), :])
                    cols = slice((n * share + r) * lanes, (n * share + r + 1) * lanes)
                    out[p * half : (p + 1) * half, cols] = jnp.concatenate(parts, axis=0).astype(BF16)


def contract(places, blocks, tables, n_grp, split, row_blocks, rank):
    slots, edge, width = blocks.shape
    half, lanes = edge // 2, 2 * rank
    part = rank // (n_grp * split) * lanes
    shapes = [
        jax.ShapeDtypeStruct((row_blocks * half, part * len(pieces)), BF16)
        for pieces in reduce_layout(n_grp, split, 0)
    ]
    factor_rows = sum(table.shape[0] * table.shape[1] for table in tables)
    flops = 2 * slots * edge * width * 4 * edge + 2 * row_blocks * rank * slots * edge * edge * rank
    floats = [
        (edge * factor_rows, lanes),
        (slots * edge * half, lanes),
        (row_blocks * rank * half, lanes),
        (slots * edge, row_blocks * rank),
    ]
    held = 2 * blocks.size + sum(4 * rows * columns for rows, columns in floats)
    far = pl.BlockSpec(memory_space=pltpu.HBM)
    return pl.pallas_call(
        functools.partial(
            contract_kernel,
            n_tables=len(tables),
            n_grp=n_grp,
            split=split,
            n_outs=len(shapes),
            slots=slots,
            row_blocks=row_blocks,
            edge=edge,
            rank=rank,
        ),
        in_specs=[far] * 2 + [VMEM] * len(tables),
        out_specs=[VMEM] * len(shapes),
        out_shape=shapes,
        scratch_shapes=[
            pltpu.SMEM(places.shape, jnp.int32),
            pltpu.VMEM(blocks.shape, BF16),
            *(pltpu.VMEM(shape, F32) for shape in floats),
            pltpu.SemaphoreType.DMA((1,)),
            pltpu.SemaphoreType.DMA((slots,)),
        ],
        compiler_params=params(max(held + 8 * 1024 * 1024, 50 * 1024 * 1024)),
        cost_estimate=pl.CostEstimate(
            flops=flops, bytes_accessed=2 * blocks.size + 4 * row_blocks * edge * rank * rank, transcendentals=0
        ),
        name="contract",
    )(places, blocks, *tables)


def project_kernel(*refs, sides, rank):
    pieces, olds, panel, out = refs[: -sides - 2], refs[-sides - 2 : -2], refs[-2], refs[-1]
    count = len(pieces) // sides
    width = panel.shape[1]
    lanes = 2 * rank
    totals, lefts = [], []
    for d in range(sides):
        total = pieces[d * count][:, :width].astype(F32)
        for piece in pieces[d * count + 1 : (d + 1) * count]:
            total = total + piece[:, :width].astype(F32)
        totals.append(total.astype(BF16))
        lefts.append(olds[d][:, olds[d].shape[1] - lanes :])
    total = jnp.concatenate(totals, axis=0)
    panel[...] = total
    left = jnp.concatenate(lefts, axis=0).astype(F32).T.astype(BF16)
    both = jnp.dot(left, total, preferred_element_type=F32)
    low = lax.broadcasted_iota(jnp.int32, (rank, lanes), 1) < rank
    sums = []
    for r in range(width // lanes):
        cols = slice(r * lanes, (r + 1) * lanes)
        own = jnp.where(low, both[:rank, cols], both[rank:, cols])
        sums.append(own + pltpu.roll(own, rank, 1))
    for r in range(0, len(sums), 2):
        out[:, r // 2 * lanes : (r // 2 + 1) * lanes] = jnp.where(low, sums[r], sums[r + 1]).astype(out.dtype)


def project(olds, pieces, rank, kind):
    sides = len(olds)
    height, width = pieces[0].shape
    shapes = [
        jax.ShapeDtypeStruct((height * sides, width), BF16),
        jax.ShapeDtypeStruct((rank, width // 2), kind),
    ]
    return pl.pallas_call(
        functools.partial(project_kernel, sides=sides, rank=rank),
        in_specs=[VMEM] * (sides + len(pieces)),
        out_specs=[VMEM] * 2,
        out_shape=shapes,
        compiler_params=params(24 * 1024 * 1024),
        name="project",
    )(*pieces, *olds)


def rows_kernel(panel, *refs, rank):
    pieces, out = refs[:-1], refs[-1]
    lanes = 2 * rank
    total = pieces[0][...].astype(F32)
    for piece in pieces[1:]:
        total = total + piece[...].astype(F32)
    low = lax.broadcasted_iota(jnp.int32, (rank, lanes), 1) < rank
    zero = jnp.zeros((rank, lanes), F32)
    upper, lower = [], []
    for r in range(total.shape[1] // lanes):
        value = total[:, r * lanes : (r + 1) * lanes]
        turned = pltpu.roll(value, rank, 1)
        upper += [jnp.where(low, value, zero).astype(BF16), jnp.where(low, turned, zero).astype(BF16)]
        lower += [jnp.where(low, zero, turned).astype(BF16), jnp.where(low, zero, value).astype(BF16)]
    right = jnp.concatenate([jnp.concatenate(upper, axis=1), jnp.concatenate(lower, axis=1)], axis=0)
    out[...] = lax.dot_general(
        panel[...], right, (((1,), (1,)), ((), ())), preferred_element_type=F32
    ).astype(BF16)


def row_terms(panel, pieces, rank):
    return pl.pallas_call(
        functools.partial(rows_kernel, rank=rank),
        in_specs=[VMEM] * (1 + len(pieces)),
        out_specs=VMEM,
        out_shape=jax.ShapeDtypeStruct((panel.shape[0], 2 * rank), BF16),
        compiler_params=params(24 * 1024 * 1024),
        name="row_terms",
    )(panel, *pieces)


def gram_kernel(*refs, rank):
    terms, rows, gram = refs[:-2], refs[-2], refs[-1]
    height = rows.shape[0]
    if len(terms) == 1:
        total = terms[0][...]
    else:
        own = terms[0][:height, :] + terms[1][height:, :]
        total = jnp.concatenate([own, terms[0][height:, :] + terms[1][:height, :]], axis=0)
    rows[...] = total[:height, :]
    full = jnp.dot(total.T, total, precision=lax.Precision.HIGHEST, preferred_element_type=F32)
    square = full[:rank, :rank] + full[rank:, rank:]
    gram[...] = jnp.concatenate([square[: rank // 2, :], square[rank // 2 :, :]], axis=1)


def gram_terms(terms, rank):
    height, lanes = terms[0].shape
    shapes = [
        jax.ShapeDtypeStruct((height // len(terms), lanes), F32),
        jax.ShapeDtypeStruct((rank // 2, lanes), F32),
    ]
    return pl.pallas_call(
        functools.partial(gram_kernel, rank=rank),
        in_specs=[VMEM] * len(terms),
        out_specs=[VMEM] * 2,
        out_shape=shapes,
        compiler_params=params(24 * 1024 * 1024),
        name="gram_terms",
    )(*terms)


def finish_kernel(*refs, rows_total):
    pieces, rows, new_rows, gram = refs[:-3], refs[-3], refs[-2], refs[-1]
    total = pieces[0][...]
    for piece in pieces[1:]:
        total = total + piece[...]
    rank = gram.shape[0]
    total = jnp.concatenate([total[:, :rank], total[:, rank:]], axis=0)
    square = total.shape
    diagonal = lax.broadcasted_iota(jnp.int32, square, 0) == lax.broadcasted_iota(jnp.int32, square, 1)
    trace = jnp.sum(jnp.where(diagonal, total, 0.0), axis=1, keepdims=True)
    trace = jnp.sum(trace, axis=0, keepdims=True)
    gram[...] = total * (rank / trace)
    scale = lax.rsqrt(trace / (rows_total * rank))
    row_blocks = new_rows.shape[0]
    lanes = 2 * rank
    half = rows.shape[0] // row_blocks
    pairs = half // 2
    low = lax.broadcasted_iota(jnp.int32, (pairs, lanes), 1) < rank
    for p in range(row_blocks):
        even = rows[pl.ds(p * half, pairs, stride=2), :] * scale
        odd = rows[pl.ds(p * half + 1, pairs, stride=2), :] * scale
        lower = jnp.where(low, even, pltpu.roll(odd, rank, 1))
        upper = jnp.where(low, pltpu.roll(even, rank, 1), odd)
        for q, value in enumerate((lower, upper)):
            for i in range(pairs):
                at = (q * pairs + i) * lanes
                new_rows[p : p + 1, at : at + lanes] = value[i : i + 1, :]


def finish(pieces, rows, row_blocks, rows_total):
    rank = pieces[0].shape[1] // 2
    shapes = [
        jax.ShapeDtypeStruct((row_blocks, rows.size // row_blocks), F32),
        jax.ShapeDtypeStruct((rank, rank), F32),
    ]
    return pl.pallas_call(
        functools.partial(finish_kernel, rows_total=rows_total),
        in_specs=[VMEM] * (len(pieces) + 1),
        out_specs=[VMEM] * 2,
        out_shape=shapes,
        compiler_params=params(24 * 1024 * 1024),
        name="finish",
    )(*pieces, rows)


def two_step(n_grp, split):
    return n_grp == 4 and split == 2


def reduce_layout(n_grp, split, core):
    if not two_step(n_grp, split):
        return [[(m, h) for h in range(split)] for m in range(n_grp)]
    near, side = 1 + core, 2 - core
    other = 1 - core
    return [
        [(near, core), (3, core)],
        [(side, other), (3, other)],
        [(side, core)],
        [(0, core), (0, other), (near, other)],
    ]


def reduce_panel(shares, old, n_grp, n_dev, split):
    if not two_step(n_grp, split):
        width = shares[0].shape[1] // split
        parts = [shares[0]] + [swap(shares[m], "grp", n_grp, m) for m in range(1, n_grp)]
        if split == 1:
            return [old], parts
        core = lax.axis_index("dev") % split

        def side(i):
            at = (core + i) % split * width
            return [lax.dynamic_slice_in_dim(part, at, width, 1) for part in parts]

        total = sum(part.astype(F32) for part in side(1)).astype(BF16)
        crossed = swap(jnp.concatenate([total, old], axis=1), "dev", n_dev, 1)
        own = sum(part.astype(F32) for part in side(0)).astype(BF16)
        return [old, crossed], [own, crossed]

    def send(x, own, cross):
        pairs = []
        for g in range(n_grp):
            for d in range(n_dev):
                core = d % 2
                mask = 1 + core if own else 2 - core
                pairs.append((g * n_dev + d, (g ^ mask) * n_dev + (d ^ cross)))
        return lax.ppermute(x, ("grp", "dev"), pairs)

    width = shares[0].shape[1] // 2
    first = send(shares[0], True, 0).astype(F32)
    second = send(shares[1], False, 0).astype(F32)
    own = send((shares[2].astype(F32) + first[:, width:]).astype(BF16), False, 0)
    rest = [shares[3][:, i * width : (i + 1) * width].astype(F32) for i in range(3)]
    other = send((rest[2] + second[:, width:]).astype(BF16), True, 1)
    crossed = (rest[1] + second[:, :width]).astype(BF16)
    crossed = swap(jnp.concatenate([crossed, old], axis=1), "dev", n_dev, 1)
    kept = (rest[0] + first[:, :width]).astype(BF16)
    return [old, crossed], [kept, own, other, crossed]


def body(blocks, coords, counts, row_place, factor_one, factor_two, factor_three):
    edge = blocks.shape[1]
    rank = factor_one.shape[1] // edge
    row_blocks = factor_one.shape[0]
    n_grp, n_dev = lax.axis_size("grp"), lax.axis_size("dev")
    direct = is_direct(n_dev)
    split = 2 if direct else 1
    far = far_masks(n_dev)

    def sibling(x):
        return swap(x, "dev", n_dev, 1)

    def over_grp(pieces):
        return pieces[:1] + [swap(pieces[m], "grp", n_grp, m) for m in range(n_grp - 1, 0, -1)]

    packed = jnp.concatenate([factor_two, factor_three], axis=0)
    if direct:
        tables = [jnp.stack([packed] + [swap(packed, "dev", n_dev, m) for m in far])]
        tables.append(sibling(tables[0]))
    else:
        tables = [lax.all_gather(packed, "dev", axis=0)]
    hits = coords[:, :, None] == jnp.arange(row_place.shape[0])[None, None, :]
    places = jnp.sum(jnp.where(hits, row_place[None, None, :], 0), axis=2)
    live = jnp.arange(coords.shape[1])[None, :] < counts[0]
    row = jnp.where(live, places % row_blocks, row_blocks)
    places = jnp.where(jnp.arange(coords.shape[0])[:, None] == 0, row, places)
    shares = list(contract(places, blocks, tables, n_grp, split, row_blocks, rank))
    factor_one, shares[0] = lax.optimization_barrier((factor_one, shares[0]))
    old = factor_one.reshape(row_blocks, 2, edge // 2, rank).transpose(0, 2, 1, 3)
    old = old.reshape(row_blocks * edge // 2, 2 * rank)
    olds, pieces = reduce_panel(shares, old, n_grp, n_dev, split)
    panel, proj = project(olds, pieces, rank, BF16 if direct else F32)
    if direct:
        projs = [proj] + [swap(proj, "dev", n_dev, m) for m in far]
    else:
        projs = [lax.psum(proj, "dev")]
    terms = row_terms(panel, projs, rank)
    rows = sum(part.astype(F32) for part in over_grp([terms] * n_grp))
    rows, gram_local = gram_terms([rows, sibling(rows)] if direct else [rows], rank)
    if direct:
        grams = [gram_local] + [swap(gram_local, "dev", n_dev, m) for m in far]
    else:
        grams = [lax.psum(gram_local, "dev")]
    return tuple(finish(grams, rows, row_blocks, row_blocks * edge * n_dev))


def solution(mesh):
    placed = (
        P(("grp", "dev"), None, None),
        P(None, ("grp", "dev")),
        P(("grp", "dev")),
        P(),
        P("dev", None),
        P("dev", None),
        P("dev", None),
    )
    return jax.shard_map(
        body, mesh=mesh, in_specs=placed, out_specs=(P("dev", None), P()), check_vma=False
    )
```
